32 devices in a mesh: dp: 4 (over y, x), expert: 8 (over z, core).
Axes of the slice: x: 2, y: 2, z: 4, core: 2. Of those that a mesh axis runs over, the one named last changes fastest.
Arguments:
- tokens: bfloat16 [4096, 2560], P(('dp', 'expert')), may hold values from -6 to 6
- cotangent: bfloat16 [4096, 2560], P(('dp', 'expert')), may hold values from -6 to 6
- routes: int32 [4096, 2], P(('dp', 'expert')), may hold values from 0 to 3, all different within a row; in each aligned block of 128 rows (0 to 127, 128 to 255, ...) at most 80 rows name the same one
- gate_values: float32 [4096, 2], P(('dp', 'expert')), may hold values from 0.1 to 1
- up_weight: bfloat16 [8, 2560, 384], P('expert', 'dp'), may hold values from -0.125 to 0.125
- down_weight: bfloat16 [8, 2560, 384], P('expert', 'dp'), may hold values from -0.21875 to 0.21875
Outputs:
- grad_tokens: bfloat16 [4096, 2560], P(('dp', 'expert'))
- grad_up: bfloat16 [8, 2560, 384], P('expert', 'dp')
- grad_down: bfloat16 [8, 2560, 384], P('expert', 'dp')
The draws below stay inside these ranges and needn't reach their ends.
Inputs may be any that keep to these rules, and one draw needn't show every extreme that they name: `routes`: each row names 2 different experts. Among the rows of one device no expert is named by more than 80 rows, a bound that some block reaches.
All inputs are finite; a program needn't handle non-finite values.
Results may differ from the reference program's by a relative error of at most 0.023.
Values may be sent and summed in bfloat16 or wider, within the bound.
No kernel may reach another device: no remote copies, remote signals or barrier semaphores. Data moves between devices by JAX's collectives and lax.ppermute only.
A program may use at most 64 MiB of HBM per device.

```python
import math
import jax
import jax.numpy as jnp
import numpy as np
from jax import lax

D = 2560
FF = 768
TOP = 2
TOK_DEV = 128
FH = 384
EXPERTS = 4
SLOTS = 8
CAP = 80
TOKENS = 4096
N_DP = 4
N_EXPERT = 8


def block_levels(rng, dims, pieces, low, largest):
    level, own = 1.0, jax.random.fold_in(rng, 6)
    for dim, shards_of in pieces:
        draws = jnp.exp(jax.random.uniform(jax.random.fold_in(own, dim), (shards_of,), jnp.float32, low / len(pieces), largest / len(pieces)))
        level = level * jnp.repeat(draws, dims[dim] // shards_of).reshape([-1 if axis == dim else 1 for axis in range(len(dims))])
    return level


def deal_out(stream_key, own, number, rows, number_of, top, bound, slope):
    sequence = jax.random.permutation(stream_key, number_of)
    packed, ordinary = portions_of(number_of, rows * top, bound, slope, True), portions_of(number_of, rows * top, bound, slope, False)
    places = jnp.arange(number_of)

    def named(tallies, offset_by):
        used = int((tallies > 0).sum())
        fixed = max(1, used // 4)
        moved = fixed + (places - fixed + offset_by * (used - fixed)) % max(1, number_of - fixed)
        return jnp.zeros((number_of,), jnp.int32).at[sequence[jnp.where(places < fixed, places, moved)]].set(jnp.asarray(tallies, jnp.int32))

    tallies = jnp.where(number % 4 == 0, named(packed, number // 4), named(ordinary, number - number // 4 - 1))
    mixed = jax.random.permutation(jax.random.fold_in(own, 3), number_of)
    giver, sink = mixed[0:number_of // 2 * 2:2], mixed[1:number_of // 2 * 2:2]
    room = jnp.minimum(tallies[giver] - 1, bound - tallies[sink]) // 2
    room = jnp.where((giver == sequence[0]) | (sink == sequence[0]) | (tallies[sink] == 0), 0, jnp.maximum(room, 0))
    moved = jax.random.randint(jax.random.fold_in(own, 4), (number_of // 2,), 0, 1 << 20) % (room + 1)
    tallies = tallies.at[giver].add(-moved).at[sink].add(moved)
    members = jnp.searchsorted(jnp.cumsum(tallies), jnp.arange(rows * top), side="right").astype(jnp.int32)
    listing = members.reshape(top, rows).T
    listing = listing[jax.random.permutation(jax.random.fold_in(own, 1), rows)]
    offset_by = jax.random.randint(jax.random.fold_in(own, 2), (rows, 1), 0, top)
    return jnp.take_along_axis(listing, (jnp.arange(top)[None, :] + offset_by) % top, axis=1)


def portions_of(amount, total, reach, lean, full):
    portions = [(1 << 20) // math.isqrt(standing ** lean) + 1 for standing in range(1, amount + 1)]
    largest = reach if full else min(reach, max(-(-total // amount), total * portions[0] // sum(portions)))
    least = 1 if total - largest >= amount - 1 else 0
    counts, spare = [largest] + [least] * (amount - 1), total - largest - least * (amount - 1)
    while spare > 0:
        candidates = [i for i in range(1, amount) if counts[i] < largest] or [i for i in range(1, amount) if counts[i] < reach]
        whole, remaining = sum([portions[i] for i in candidates]), spare
        for i in candidates:
            extra = min(reach - counts[i], max(1, remaining * portions[i] // whole), spare)
            counts[i] = counts[i] + extra
            spare = spare - extra
    return np.array(counts)


def normal_values(stream_key, dims, spread, limit, pieces=(), kind=jnp.bfloat16):
    values = spread * jax.random.normal(stream_key, dims, jnp.float32)
    if pieces:
        values = values * block_levels(stream_key, dims, pieces, -0.22, 0.18)
    return jnp.clip(values, -limit, limit).astype(kind)


def setup_inputs(seed: int = 0) -> dict:
    key_list = jax.random.split(jax.random.key(seed), 7)
    tokens = normal_values(key_list[0], (TOKENS, D), 1.0, 6.0, ((0, 32),))
    cotangent = normal_values(key_list[1], (TOKENS, D), 1.0, 6.0, ((0, 32),))
    routes_keys = jax.random.split(jax.random.fold_in(key_list[2], 1), TOKENS // TOK_DEV)
    routes_turns = jax.random.permutation(jax.random.fold_in(key_list[2], 3), TOKENS // TOK_DEV)
    routes = jax.vmap(lambda own, number: deal_out(jax.random.fold_in(key_list[2], 2), own, number, TOK_DEV, EXPERTS, TOP, CAP, 2))(routes_keys, routes_turns).reshape((TOKENS, TOP))
    gate_values = jnp.clip(0.1 + 0.9 * jax.random.uniform(key_list[3], (TOKENS, TOP), jnp.float32) ** block_levels(key_list[3], (TOKENS, TOP), ((0, 32),), -0.2, 0.2), 0.1, 1.0)
    up_weight = normal_values(key_list[4], (SLOTS, D, FH), D ** -0.5, 0.125, ((0, 8), (1, 4)))
    down_weight = normal_values(key_list[5], (SLOTS, D, FH), FF ** -0.5, 0.21875, ((0, 8), (1, 4)))
    return dict(tokens=tokens, cotangent=cotangent, routes=routes, gate_values=gate_values, up_weight=up_weight, down_weight=down_weight)


def plan_block(route_row, gate_row):
    onehot = (route_row[:, None] == jnp.arange(EXPERTS, dtype=jnp.int32)[None, :]).astype(jnp.int32)
    position = jnp.sum((jnp.cumsum(onehot, axis=0) - onehot) * onehot, axis=1).astype(jnp.int32)
    slot_index = (route_row.astype(jnp.int32) * CAP + position).astype(jnp.int32)
    owners = (jnp.arange(route_row.shape[0], dtype=jnp.int32) // TOP).astype(jnp.int32)
    row_table = jnp.full((EXPERTS * CAP,), TOK_DEV, jnp.int32).at[slot_index].set(owners)
    gate_table = jnp.zeros((EXPERTS * CAP,), jnp.float32).at[slot_index].set(gate_row.astype(jnp.float32))
    return slot_index, row_table, gate_table


def activation(hidden):
    sigmoid_h = jax.nn.sigmoid(hidden)
    return hidden * sigmoid_h, sigmoid_h * (1.0 + hidden * (1.0 - sigmoid_h))


def expert_pass(operands):
    rows_x, rows_s, weight_up, weight_down = operands
    hidden = jnp.dot(rows_x, weight_up, preferred_element_type=jnp.float32)
    active, slope_term = activation(hidden)
    active = active.astype(jnp.bfloat16)
    back_act = jnp.dot(rows_s, weight_down, preferred_element_type=jnp.float32)
    back_hidden = (back_act * slope_term).astype(jnp.bfloat16)
    halves = []
    for half_index in range(2):
        columns = slice(half_index * FH, (half_index + 1) * FH)
        product = lax.dot_general(back_hidden[:, columns], weight_up[:, columns], (((1,), (1,)), ((), ())), preferred_element_type=jnp.float32)
        halves.append(product.astype(jnp.bfloat16))
    grad_up = lax.dot_general(rows_x, back_hidden, (((0,), (0,)), ((), ())), preferred_element_type=jnp.float32).astype(jnp.bfloat16)
    grad_down = lax.dot_general(rows_s, active, (((0,), (0,)), ((), ())), preferred_element_type=jnp.float32).astype(jnp.bfloat16)
    return jnp.stack(halves), grad_up, grad_down


def select_rows(source_rows, row_table):
    return source_rows[row_table]


def reference(tokens, cotangent, routes, gate_values, up_weight, down_weight):
    sources = N_EXPERT
    grid_x = tokens.reshape(N_DP, sources, TOK_DEV, D)
    grid_dy = cotangent.reshape(N_DP, sources, TOK_DEV, D)
    grid_routes = routes.reshape(N_DP, sources, TOK_DEV * TOP)
    grid_gates = gate_values.reshape(N_DP, sources, TOK_DEV * TOP)
    slot_groups, tables, gate_tabs = jax.vmap(jax.vmap(plan_block))(grid_routes, grid_gates)
    up_full = up_weight.reshape(EXPERTS, 2, D, FH).transpose(0, 2, 1, 3).reshape(EXPERTS, D, FF)
    down_full = down_weight.reshape(EXPERTS, 2, D, FH).transpose(0, 2, 1, 3).reshape(EXPERTS, D, FF)

    def group_step(totals, operands):
        block_x, block_dy, slot_group, table_group, gate_group = operands
        zero_row = jnp.zeros((sources, 1, D), jnp.bfloat16)
        padded_x = jnp.concatenate([block_x, zero_row], axis=1)
        padded_dy = jnp.concatenate([block_dy, zero_row], axis=1)
        send_x = jax.vmap(select_rows)(padded_x, table_group)
        send_s = (gate_group[:, :, None] * jax.vmap(select_rows)(padded_dy, table_group).astype(jnp.float32)).astype(jnp.bfloat16)
        per_x = send_x.reshape(sources, EXPERTS, CAP, D).transpose(1, 0, 2, 3).reshape(EXPERTS, sources * CAP, D)
        per_s = send_s.reshape(sources, EXPERTS, CAP, D).transpose(1, 0, 2, 3).reshape(EXPERTS, sources * CAP, D)
        partials, grad_up, grad_down = lax.map(expert_pass, (per_x, per_s, up_full, down_full))
        by_source = partials.reshape(EXPERTS, 2, sources, CAP, D).transpose(2, 0, 3, 1, 4).reshape(sources, EXPERTS * CAP, 2, D)
        gathered = jax.vmap(select_rows)(by_source, slot_group)
        paired = jnp.sum(gathered.astype(jnp.float32), axis=2).astype(jnp.bfloat16)
        paired = lax.optimization_barrier(paired)
        summed = jnp.sum(paired.astype(jnp.float32).reshape(sources, TOK_DEV, TOP, D), axis=2)
        new_totals = (totals[0] + grad_up.astype(jnp.float32), totals[1] + grad_down.astype(jnp.float32))
        return new_totals, summed.astype(jnp.bfloat16)

    initial = (jnp.zeros((EXPERTS, D, FF), jnp.float32), jnp.zeros((EXPERTS, D, FF), jnp.float32))
    totals, grads_x = lax.scan(group_step, initial, (grid_x, grid_dy, slot_groups, tables, gate_tabs))

    def to_slots(summed_full):
        return summed_full.astype(jnp.bfloat16).reshape(EXPERTS, D, 2, FH).transpose(0, 2, 1, 3).reshape(SLOTS, D, FH)

    return grads_x.reshape(TOKENS, D), to_slots(totals[0]), to_slots(totals[1])
```

```python
import functools

import jax
import jax.numpy as jnp
from jax import lax
from jax.experimental import pallas as pl
from jax.experimental.pallas import tpu as pltpu
from jax.sharding import PartitionSpec as P

BF = jnp.bfloat16
F32 = jnp.float32
MIB = 1024 * 1024


def vmem():
    return pl.BlockSpec(memory_space=pltpu.VMEM)


def hbm():
    return pl.BlockSpec(memory_space=pl.ANY)


def params(mebibytes):
    return pltpu.CompilerParams(vmem_limit_bytes=mebibytes * MIB)


def cost(microseconds):
    return pl.CostEstimate(
        flops=int(microseconds * 1.0e9), bytes_accessed=2**20, transcendentals=0
    )


def array(*shape):
    return jax.ShapeDtypeStruct(shape, BF)


def contract(a, b, da, db):
    return lax.dot_general(a, b, (((da,), (db,)), ((), ())), preferred_element_type=F32)


def slot_plan(routes):
    tokens = routes.shape[1]
    first, second = routes[0:1, :], routes[1:2, :]
    expert = lax.broadcasted_iota(jnp.int32, (128, tokens), 0)
    named = jnp.where((expert == first) | (expert == second), 1.0, 0.0).astype(BF)
    earlier = lax.broadcasted_iota(jnp.int32, (tokens, tokens), 0)
    later = lax.broadcasted_iota(jnp.int32, (tokens, tokens), 1)
    place = contract(named, jnp.where(earlier < later, 1.0, 0.0).astype(BF), 1, 0)
    return first, second, expert, place


def slot_masks(plan, chosen, cap):
    first, second, expert, place = plan
    own = jnp.sum(jnp.where(expert == chosen, place, 0.0), axis=0, keepdims=True)
    slot = lax.broadcasted_iota(jnp.int32, (cap, first.shape[1]), 0)
    here = slot == own.astype(jnp.int32)
    return here & (first == chosen), here & (second == chosen)


def dispatch_kernel(experts, cap, shifts, moved, *refs):
    refs = list(refs)
    sources, refs = refs[: 4 + moved], refs[4 + moved :]
    moved_outs, outs, refs = refs[:moved], refs[moved : moved + len(shifts)], refs[moved + len(shifts) :]
    routes_ref, gates_ref, tok_ref, cot_ref, made, held, sems = refs
    landings = [routes_ref, gates_ref, tok_ref, cot_ref] + [held.at[i] for i in range(moved)]
    copies = []

    def copy(source, landing):
        copies.append(pltpu.make_async_copy(source, landing, sems.at[len(copies)]))
        copies[-1].start()

    for source, landing in zip(sources, landings):
        copy(source, landing)
    for one in copies[:2]:
        one.wait()
    chip = lax.axis_index("expert") // 2
    plan = slot_plan(routes_ref[...])
    gates = gates_ref[...]
    for one in copies[2:4]:
        one.wait()
    for index, shift in enumerate(shifts):
        mask0, mask1 = slot_masks(plan, lax.rem(chip + shift, experts), cap)
        gate = jnp.sum(
            jnp.where(mask0, gates[0:1, :], 0.0) + jnp.where(mask1, gates[1:2, :], 0.0),
            axis=1,
            keepdims=True,
        )
        pick = jnp.where(mask0 | mask1, 1.0, 0.0).astype(BF)
        made[index, :cap, :] = contract(pick, tok_ref[...], 1, 0).astype(BF)
        made[index, cap:, :] = (gate * contract(pick, cot_ref[...], 1, 0)).astype(BF)
        copy(made.at[index], outs[index])
    for index in range(moved):
        copies[4 + index].wait()
        copy(held.at[index], moved_outs[index])
    for one in copies[4 + moved :]:
        one.wait()


def combine_kernel(experts, cap, routes_ref, *rest):
    backs, out_ref, mark_ref = rest[:-2], rest[-2], rest[-1]
    mark_ref[...] = jnp.zeros_like(mark_ref)
    chip = lax.axis_index("expert") // 2
    plan = slot_plan(routes_ref[...])
    picks = []
    for shift in range(experts):
        mask0, mask1 = slot_masks(plan, lax.rem(chip + shift, experts), cap)
        picks.append(jnp.where(mask0 | mask1, 1.0, 0.0).astype(BF).T)
    width = out_ref.shape[1]
    tile = 640
    for start in range(0, width, tile):
        cols = slice(start, start + tile)
        total = None
        for shift in range(experts):
            term = contract(picks[shift], backs[shift][:, cols], 1, 0)
            total = term if total is None else total + term
        out_ref[:, cols] = total.astype(BF)


def chunk_rows(cap, owns, sibs, rows_x, rows_s):
    for index, block in enumerate(list(owns) + list(sibs)):
        place = slice(index * cap, (index + 1) * cap)
        rows_x[place, :] = block[:cap, :]
        rows_s[place, :] = block[cap:, :]


def expert_work(rows_x, rows_s, up, down):
    hidden = contract(rows_x[...], up[...], 1, 0)
    sig = jax.nn.sigmoid(hidden)
    active = (hidden * sig).astype(BF)
    slope = sig * (1.0 + hidden * (1.0 - sig))
    back_hidden = (contract(rows_s[...], down[...], 1, 0) * slope).astype(BF)
    return active, back_hidden


def tiles(width):
    tile = 512 if width % 512 == 0 else 128
    return [slice(start, start + tile) for start in range(0, width, tile)]


def partial_rows(back_hidden, up_turned, part_own, part_sib):
    half_rows = part_own.shape[0]
    for cols in tiles(part_own.shape[1]):
        part = contract(back_hidden, up_turned[:, cols], 1, 0).astype(BF)
        part_own[:, cols] = part[:half_rows]
        part_sib[:, cols] = part[half_rows:]


def first_kernel(cap, count, layout, n_dp, *refs):
    owns, sibs, refs = refs[:count], refs[count : 2 * count], refs[2 * count :]
    n_up, n_down = len(layout[0]), len(layout[1])
    ups, downs = refs[:n_up], refs[n_up : n_up + n_down]
    part_own, part_sib, grads, up, up_turned, down, rows_x, rows_s = refs[n_up + n_down :]
    step, half = ups[0].shape
    me = lax.axis_index("dp")
    for full, lay, blocks in ((up, layout[0], ups), (down, layout[1], downs)):
        for peers, block in zip(lay, blocks):
            for place, peer in enumerate(peers):
                home = pl.ds(pl.multiple_of((me ^ peer) * step, 16), step)
                full[home, :] = block[place * step : (place + 1) * step, :]
    up_turned[...] = up[...].T
    chunk_rows(cap, owns, sibs, rows_x, rows_s)
    active, back_hidden = expert_work(rows_x, rows_s, up, down)
    for base, units, rows in ((0, back_hidden, rows_x), (half, active, rows_s)):
        turned = units.T
        for owner in range(n_dp):
            cols = slice(owner * step, (owner + 1) * step)
            grads[owner, base : base + half, :] = contract(turned, rows[:, cols], 1, 0).astype(BF)
    partial_rows(back_hidden, up_turned, part_own, part_sib)


def late_kernel(cap, count, n_dp, named, *refs):
    owns, sibs, refs = refs[:count], refs[count : 2 * count], refs[2 * count :]
    up, up_turned, down = refs[:3]
    refs = refs[3 + named :]
    part_own, part_sib, outs = refs[0], refs[1], refs[2 : 2 + n_dp]
    rows_x, rows_s = refs[2 + n_dp :]
    half = up_turned.shape[0]
    step = (outs[0].shape[1] - 4 * half) // 2
    rows = outs[0].shape[0]
    me = lax.axis_index("dp")
    chunk_rows(cap, owns, sibs, rows_x, rows_s)
    active, back_hidden = expert_work(rows_x, rows_s, up, down)
    for peer, out in enumerate(outs):
        cols = pl.ds(pl.multiple_of((me ^ peer) * step, 128), step)
        out[:, :step] = rows_x[:rows, cols]
        out[:, step : 2 * step] = rows_s[:rows, cols]
        first = 2 * step
        for units in (back_hidden, active):
            for place in (slice(0, rows), slice(rows, 2 * rows)):
                out[:, first : first + half] = units[place]
                first += half
    partial_rows(back_hidden, up_turned, part_own, part_sib)


def pair_kernel(cap, counts, *refs):
    outs = refs[len(refs) - sum(counts) :]
    place = 0
    for group, count in enumerate(counts):
        own_ref, other_ref = refs[2 * group : 2 * group + 2]
        for index in range(count):
            rows = slice(index * cap, (index + 1) * cap)
            outs[place][...] = (
                own_ref[rows, :].astype(F32) + other_ref[rows, :].astype(F32)
            ).astype(BF)
            place += 1


def pass_kernel(*refs):
    pass


def share_kernel(*refs):
    blocks, out = refs[:-1], refs[-1]
    rows = blocks[0].shape[0]
    for index, block in enumerate(blocks):
        out[index * rows : (index + 1) * rows, :] = block[:, : out.shape[1]]


def last_kernel(n_dp, *refs):
    near, blocks, shared = refs[0], refs[1 : 1 + n_dp], refs[1 + n_dp]
    out_up, out_down, rows, units = refs[-4:]
    step, half = rows.shape[1], units.shape[1]
    count = blocks[0].shape[0]
    for base, out in ((0, out_up), (1, out_down)):
        cols = slice(base * step, (base + 1) * step)
        first = 2 * step + 2 * base * half
        for index, block in enumerate(blocks):
            place = slice(2 * index * count, (2 * index + 1) * count)
            rows[place, :] = block[:, cols]
            units[place, :] = block[:, first : first + half]
            place = slice((2 * index + 1) * count, (2 * index + 2) * count)
            rows[place, :] = shared[index * count : (index + 1) * count, cols]
            units[place, :] = block[:, first + half : first + 2 * half]
        total = contract(units[...].T, rows[...], 1, 0)
        total = total + near[base * half : (base + 1) * half, :].astype(F32)
        out[0] = total.T.astype(BF)


def on_device(n_dp, n_expert, tokens, cotangent, routes, gate_values, up_weight, down_weight):
    rows, width = tokens.shape
    top = routes.shape[1]
    experts = n_expert // 2
    cap = -(-(5 * rows * top // (4 * experts)) // 16) * 16
    step, half = up_weight.shape[1:]
    bits = n_dp.bit_length() - 1
    orders = (list(range(bits)), list(range(bits))[::-1])

    def shifted(value, shift):
        pairs = [
            (2 * z + c, 2 * ((z + shift) % experts) + c) for z in range(experts) for c in range(2)
        ]
        return lax.ppermute(value, "expert", pairs)

    def swapped(value):
        return lax.ppermute(value, "expert", [(i, i ^ 1) for i in range(n_expert)])

    def across(value, bit):
        return lax.ppermute(value, "dp", [(d, d ^ (1 << bit)) for d in range(n_dp)])

    routes_t, gates_t = routes.T, gate_values.T

    def dispatch(shifts, *moved):
        return pl.pallas_call(
            functools.partial(dispatch_kernel, experts, cap, shifts, len(moved)),
            out_shape=[array(*value.shape) for value in moved]
            + [array(2 * cap, width)] * len(shifts),
            in_specs=[hbm()] * (4 + len(moved)),
            out_specs=[hbm()] * (len(moved) + len(shifts)),
            scratch_shapes=[
                pltpu.VMEM(routes_t.shape, routes_t.dtype),
                pltpu.VMEM(gates_t.shape, gates_t.dtype),
                pltpu.VMEM(tokens.shape, BF),
                pltpu.VMEM(cotangent.shape, BF),
                pltpu.VMEM((len(shifts), 2 * cap, width), BF),
                pltpu.VMEM((len(moved), *moved[0].shape), BF),
                pltpu.SemaphoreType.DMA((4 + 2 * len(moved) + len(shifts),)),
            ],
            compiler_params=params(56),
            cost_estimate=cost(2),
            name="dispatch",
        )(routes_t, gates_t, tokens, cotangent, *moved)

    shifts = list(range(experts))
    far = experts // 2
    groups = [[shift for shift in shifts if shift != far], [far]]
    own, sib = {}, {}
    order = groups[0][1:] + [far, 0]
    up_own, down_own, *sends = dispatch(order, up_weight[0], down_weight[0])
    for shift, send in zip(order, sends):
        own[shift] = shifted(send, shift) if shift else send

    def passed(value, estimate, *after):
        return pl.pallas_call(
            pass_kernel,
            out_shape=array(*value.shape),
            in_specs=[hbm()] * (1 + len(after)),
            out_specs=hbm(),
            input_output_aliases={0: 0},
            compiler_params=params(1),
            cost_estimate=cost(estimate),
            name="after",
        )(value, *after)

    for shift in groups[0]:
        own[shift] = passed(own[shift], 8) if shift else own[shift]
        sib[shift] = swapped(own[shift])

    def gathered(weight, order):
        blocks, layout, held = [weight], [[0]], [0]
        for bit in order:
            blocks.append(
                across(jnp.concatenate(blocks) if len(blocks) > 1 else weight, bit)
            )
            layout.append([peer ^ (1 << bit) for peer in held])
            held = held + layout[-1]
        return blocks, layout

    ups, up_layout = gathered(up_own, orders[0])
    downs, down_layout = gathered(down_own, orders[1])

    def chunk_call(kernel, group, operands, outs, name, estimate):
        count = len(group)
        parts = [array(count * cap, width)] * 2
        return pl.pallas_call(
            functools.partial(kernel[0], cap, count, *kernel[1:]),
            out_shape=parts + outs,
            in_specs=[vmem()] * (2 * count + len(operands)),
            out_specs=[vmem()] * (2 + len(outs)),
            scratch_shapes=[pltpu.VMEM((2 * count * cap, width), BF)] * 2,
            compiler_params=params(20),
            cost_estimate=cost(estimate),
            name=name,
        )(*[own[shift] for shift in group], *[sib[shift] for shift in group], *operands)

    part_own, part_sib, near_grads, *weights = chunk_call(
        (first_kernel, (up_layout, down_layout), n_dp),
        groups[0],
        [*ups, *downs],
        [
            array(n_dp, 2 * half, step),
            array(width, half),
            array(half, width),
            array(width, half),
        ],
        "first",
        10,
    )
    near_grads = lax.psum_scatter(near_grads, "dp", scatter_dimension=0, tiled=True)
    halves = [(part_own, swapped(part_sib))]

    own[far] = passed(own[far], 12, part_own)
    sib[far] = swapped(own[far])

    pairs, ready = {}, {}

    def paired(groups, halves, *after):
        counts = [len(group) for group in groups]
        results = pl.pallas_call(
            functools.partial(pair_kernel, cap, counts),
            out_shape=[array(cap, width)] * sum(counts),
            in_specs=[vmem()] * (2 * len(counts)) + [hbm()] * len(after),
            out_specs=[vmem()] * sum(counts),
            compiler_params=params(16),
            cost_estimate=cost(1),
            name="pair",
        )(*[value for both in halves for value in both], *after)
        for shift, result in zip([shift for group in groups for shift in group], results):
            ready[shift] = result
            pairs[shift] = passed(shifted(result, experts - shift), 20) if shift else result

    paired(groups[:1], halves, own[far])

    named = [ready[groups[0][-1]]]
    part_own, part_sib, *blocks = chunk_call(
        (late_kernel, n_dp, len(named)),
        groups[1],
        [*weights, *named],
        [array(cap, 2 * step + 4 * half)] * n_dp,
        "late",
        4,
    )
    paired(groups[1:], [(part_own, swapped(part_sib))])

    grad_tokens, mark = pl.pallas_call(
        functools.partial(combine_kernel, experts, cap),
        out_shape=[array(rows, width), jax.ShapeDtypeStruct((8, 128), F32)],
        in_specs=[vmem()] * (1 + experts),
        out_specs=[vmem()] * 2,
        compiler_params=params(16),
        cost_estimate=cost(3),
        name="combine",
    )(routes_t, *[pairs[shift] for shift in range(experts)])

    def to_owner(value, peer):
        return lax.ppermute(value, "dp", [(d, d ^ peer) for d in range(n_dp)])

    blocks = [
        to_owner(passed(block, 0.1, ready[far]) if peer & (peer - 1) else block, peer)
        if peer
        else block
        for peer, block in enumerate(blocks)
    ]
    shared = swapped(
        pl.pallas_call(
            share_kernel,
            out_shape=array(n_dp * cap, 2 * step),
            in_specs=[vmem()] * n_dp,
            out_specs=vmem(),
            compiler_params=params(8),
            cost_estimate=cost(1),
            name="share",
        )(*blocks)
    )
    near_grads = near_grads[0]
    specs = [pl.BlockSpec(near_grads.shape, lambda i: (0, 0))]
    specs += [pl.BlockSpec(value.shape, lambda i: (0, 0)) for value in blocks + [shared]]
    specs += [pl.BlockSpec((8, 128), lambda i: (0, 0))]
    grad_up, grad_down = pl.pallas_call(
        functools.partial(last_kernel, n_dp),
        grid=(1,),
        out_shape=[array(1, step, half)] * 2,
        in_specs=specs,
        out_specs=[pl.BlockSpec((1, step, half), lambda i: (0, 0, 0))] * 2,
        scratch_shapes=[
            pltpu.VMEM((2 * n_dp * cap, step), BF),
            pltpu.VMEM((2 * n_dp * cap, half), BF),
        ],
        compiler_params=params(24),
        cost_estimate=cost(4),
        name="grads",
    )(near_grads, *blocks, shared, mark)
    return (grad_tokens, grad_up, grad_down)


def solution(mesh):
    in_specs = (
        P(("dp", "expert"), None),
        P(("dp", "expert"), None),
        P(("dp", "expert"), None),
        P(("dp", "expert"), None),
        P("expert", "dp", None),
        P("expert", "dp", None),
    )
    out_specs = (P(("dp", "expert"), None), P("expert", "dp", None), P("expert", "dp", None))
    return jax.shard_map(
        functools.partial(on_device, mesh.shape["dp"], mesh.shape["expert"]),
        mesh=mesh,
        in_specs=in_specs,
        out_specs=out_specs,
        check_vma=False,
    )
```

```python
import functools

import jax
import jax.numpy as jnp
from jax import lax
from jax.experimental import pallas as pl
from jax.experimental.pallas import tpu as pltpu
from jax.sharding import PartitionSpec as P

BF = jnp.bfloat16
F32 = jnp.float32
MIB = 1024 * 1024


def vmem():
    return pl.BlockSpec(memory_space=pltpu.VMEM)


def hbm():
    return pl.BlockSpec(memory_space=pl.ANY)


def params(mebibytes):
    return pltpu.CompilerParams(vmem_limit_bytes=mebibytes * MIB)


def cost(microseconds):
    return pl.CostEstimate(
        flops=int(microseconds * 1.0e9), bytes_accessed=2**20, transcendentals=0
    )


def array(*shape):
    return jax.ShapeDtypeStruct(shape, BF)


def contract(a, b, da, db):
    return lax.dot_general(a, b, (((da,), (db,)), ((), ())), preferred_element_type=F32)


def slot_plan(routes):
    tokens = routes.shape[1]
    first, second = routes[0:1, :], routes[1:2, :]
    expert = lax.broadcasted_iota(jnp.int32, (128, tokens), 0)
    named = jnp.where((expert == first) | (expert == second), 1.0, 0.0).astype(BF)
    earlier = lax.broadcasted_iota(jnp.int32, (tokens, tokens), 0)
    later = lax.broadcasted_iota(jnp.int32, (tokens, tokens), 1)
    place = contract(named, jnp.where(earlier < later, 1.0, 0.0).astype(BF), 1, 0)
    return first, second, expert, place


def slot_masks(plan, chosen, cap):
    first, second, expert, place = plan
    own = jnp.sum(jnp.where(expert == chosen, place, 0.0), axis=0, keepdims=True)
    slot = lax.broadcasted_iota(jnp.int32, (cap, first.shape[1]), 0)
    here = slot == own.astype(jnp.int32)
    return here & (first == chosen), here & (second == chosen)


def slot_pick(plan, gates, chosen, cap):
    mask0, mask1 = slot_masks(plan, chosen, cap)
    gate = jnp.sum(
        jnp.where(mask0, gates[0:1, :], 0.0) + jnp.where(mask1, gates[1:2, :], 0.0),
        axis=1,
        keepdims=True,
    )
    return jnp.where(mask0 | mask1, 1.0, 0.0).astype(BF), gate


def relay_x_kernel(cap, plan_ref, tok_ref, cot_ref, keep_ref, on_ref, cot_out):
    chip = lax.axis_index("expert") // 2
    values = plan_ref[...]
    plan = slot_plan(values[0:2, :].astype(jnp.int32))
    for chosen, out in ((chip, keep_ref), (chip ^ 1, on_ref)):
        pick, _ = slot_pick(plan, values[2:4, :], chosen, cap)
        out[...] = contract(pick, tok_ref[...], 1, 0).astype(BF)
    cot_out[...] = cot_ref[...]


def relay_s_kernel(cap, plan_ref, cot_ref, kept_ref, named_ref, keep_ref, on_ref):
    chip = lax.axis_index("expert") // 2
    values = plan_ref[...]
    plan = slot_plan(values[0:2, :].astype(jnp.int32))
    keep_ref[:cap, :] = kept_ref[...]
    for chosen, out, start in ((chip, keep_ref, cap), (chip ^ 1, on_ref, 0)):
        pick, gate = slot_pick(plan, values[2:4, :], chosen, cap)
        out[start : start + cap, :] = (gate * contract(pick, cot_ref[...], 1, 0)).astype(BF)


def dispatch_kernel(experts, cap, shifts, moved, *refs):
    refs = list(refs)
    sources, refs = refs[: 4 + moved], refs[4 + moved :]
    moved_outs, outs, refs = refs[:moved], refs[moved : moved + len(shifts)], refs[moved + len(shifts) :]
    routes_ref, gates_ref, tok_ref, cot_ref, made, held, sems = refs
    landings = [routes_ref, gates_ref, tok_ref, cot_ref] + [held.at[i] for i in range(moved)]
    copies = []

    def copy(source, landing):
        copies.append(pltpu.make_async_copy(source, landing, sems.at[len(copies)]))
        copies[-1].start()

    for source, landing in zip(sources, landings):
        copy(source, landing)
    for one in copies[:2]:
        one.wait()
    chip = lax.axis_index("expert") // 2
    plan = slot_plan(routes_ref[...])
    gates = gates_ref[...]
    for one in copies[2:4]:
        one.wait()
    for index, shift in enumerate(shifts):
        pick, gate = slot_pick(plan, gates, chip ^ shift, cap)
        made[index, :cap, :] = contract(pick, tok_ref[...], 1, 0).astype(BF)
        made[index, cap:, :] = (gate * contract(pick, cot_ref[...], 1, 0)).astype(BF)
        copy(made.at[index], outs[index])
    for index in range(moved):
        copies[4 + index].wait()
        copy(held.at[index], moved_outs[index])
    for one in copies[4 + moved :]:
        one.wait()


def combine_kernel(experts, cap, routes_ref, *rest):
    backs, out_ref, mark_ref = rest[:-2], rest[-2], rest[-1]
    mark_ref[...] = jnp.zeros_like(mark_ref)
    chip = lax.axis_index("expert") // 2
    plan = slot_plan(routes_ref[...])
    picks = []
    for shift in range(experts):
        mask0, mask1 = slot_masks(plan, chip ^ shift, cap)
        picks.append(jnp.where(mask0 | mask1, 1.0, 0.0).astype(BF).T)
    width = out_ref.shape[1]
    tile = 640
    for start in range(0, width, tile):
        cols = slice(start, start + tile)
        total = None
        for shift in range(experts):
            term = contract(picks[shift], backs[shift][:, cols], 1, 0)
            total = term if total is None else total + term
        out_ref[:, cols] = total.astype(BF)


def chunk_rows(cap, owns, sibs, rows_x, rows_s):
    for index, block in enumerate(list(owns) + list(sibs)):
        place = slice(index * cap, (index + 1) * cap)
        rows_x[place, :] = block[:cap, :]
        rows_s[place, :] = block[cap:, :]


def expert_work(rows_x, rows_s, up, down):
    hidden = contract(rows_x[...], up[...], 1, 0)
    sig = jax.nn.sigmoid(hidden)
    active = (hidden * sig).astype(BF)
    slope = sig * (1.0 + hidden * (1.0 - sig))
    back_hidden = (contract(rows_s[...], down[...], 1, 0) * slope).astype(BF)
    return active, back_hidden


def tiles(width):
    tile = 512 if width % 512 == 0 else 128
    return [slice(start, start + tile) for start in range(0, width, tile)]


def partial_rows(back_hidden, up_turned, part_own, part_sib):
    half_rows = part_own.shape[0]
    for cols in tiles(part_own.shape[1]):
        part = contract(back_hidden, up_turned[:, cols], 1, 0).astype(BF)
        part_own[:, cols] = part[:half_rows]
        part_sib[:, cols] = part[half_rows:]


def first_kernel(cap, count, layout, *refs):
    owns, sibs, refs = refs[:count], refs[count : 2 * count], refs[2 * count :]
    n_up, n_down = len(layout[0]), len(layout[1])
    ups, downs = refs[:n_up], refs[n_up : n_up + n_down]
    refs = refs[n_up + n_down :]
    part_own, part_sib, sum_up, sum_down, up, up_turned, down, rows_x, rows_s = refs
    step = ups[0].shape[0]
    me = lax.axis_index("dp")
    for full, lay, blocks in ((up, layout[0], ups), (down, layout[1], downs)):
        for peers, block in zip(lay, blocks):
            for place, peer in enumerate(peers):
                home = pl.ds(pl.multiple_of((me ^ peer) * step, 16), step)
                full[home, :] = block[place * step : (place + 1) * step, :]
    up_turned[...] = up[...].T
    chunk_rows(cap, owns, sibs, rows_x, rows_s)
    active, back_hidden = expert_work(rows_x, rows_s, up, down)
    partial_rows(back_hidden, up_turned, part_own, part_sib)
    for units, rows, total in ((active, rows_s, sum_down), (back_hidden, rows_x, sum_up)):
        turned = units.T
        for cols in tiles(total.shape[1]):
            total[:, cols] = contract(turned, rows[:, cols], 1, 0)


def tail_kernel(cap, count, order_up, order_down, *refs):
    x_own, s_own, x_sib, s_sib = refs[:4]
    refs = refs[4:]
    up, up_turned, down, up_in, down_in = refs[:5]
    refs = refs[6:]
    part_own, part_sib = refs[:2]
    cut = len(order_up) // 2
    up_outs, down_outs = refs[2 : 3 + cut], refs[3 + cut : 4 + 2 * cut]
    rows_x, rows_s = refs[4 + 2 * cut :]
    half, step = up_outs[1].shape
    me = lax.axis_index("dp")
    for rows, own, sib in ((rows_x, x_own, x_sib), (rows_s, s_own, s_sib)):
        rows[:cap, :] = own[...]
        rows[cap:, :] = sib[...]
    active, back_hidden = expert_work(rows_x, rows_s, up, down)
    for units, rows, before, order, outs in (
        (active, rows_s, down_in, order_down, down_outs),
        (back_hidden, rows_x, up_in, order_up, up_outs),
    ):
        turned = units.T
        for place, peer in enumerate(order):
            cols = pl.ds(pl.multiple_of((me ^ peer) * step, 128), step)
            block = (before[:, cols] + contract(turned, rows[:, cols], 1, 0)).astype(BF)
            if place < cut:
                outs[0][place * half : (place + 1) * half, :] = block
            else:
                outs[1 + place - cut][...] = block
    partial_rows(back_hidden, up_turned, part_own, part_sib)


def pair_kernel(cap, counts, *refs):
    outs = refs[len(refs) - sum(counts) :]
    place = 0
    for group, count in enumerate(counts):
        own_ref, other_ref = refs[2 * group : 2 * group + 2]
        for index in range(count):
            rows = slice(index * cap, (index + 1) * cap)
            outs[place][...] = (
                own_ref[rows, :].astype(F32) + other_ref[rows, :].astype(F32)
            ).astype(BF)
            place += 1


def pass_kernel(*refs):
    pass


def last_kernel(count, *refs):
    total = refs[0][...].astype(F32)
    for term in refs[1:count]:
        total = total + term[...].astype(F32)
    refs[-1][0] = total.T.astype(BF)


def on_device(n_dp, n_expert, tokens, cotangent, routes, gate_values, up_weight, down_weight):
    rows, width = tokens.shape
    top = routes.shape[1]
    experts = n_expert // 2
    cap = -(-(5 * rows * top // (4 * experts)) // 16) * 16
    step, half = up_weight.shape[1:]
    bits = n_dp.bit_length() - 1
    orders = (list(range(bits)), list(range(bits))[::-1])

    def shifted(value, shift):
        pairs = [(2 * z + c, 2 * (z ^ shift) + c) for z in range(experts) for c in range(2)]
        return lax.ppermute(value, "expert", pairs)

    def swapped(value):
        return lax.ppermute(value, "expert", [(i, i ^ 1) for i in range(n_expert)])

    def across(value, bit):
        return lax.ppermute(value, "dp", [(d, d ^ (1 << bit)) for d in range(n_dp)])

    routes_t, gates_t = routes.T, gate_values.T

    def dispatch(shifts, *moved):
        return pl.pallas_call(
            functools.partial(dispatch_kernel, experts, cap, shifts, len(moved)),
            out_shape=[array(*value.shape) for value in moved]
            + [array(2 * cap, width)] * len(shifts),
            in_specs=[hbm()] * (4 + len(moved)),
            out_specs=[hbm()] * (len(moved) + len(shifts)),
            scratch_shapes=[
                pltpu.VMEM(routes_t.shape, routes_t.dtype),
                pltpu.VMEM(gates_t.shape, gates_t.dtype),
                pltpu.VMEM(tokens.shape, BF),
                pltpu.VMEM(cotangent.shape, BF),
                pltpu.VMEM((len(shifts), 2 * cap, width), BF),
                pltpu.VMEM((len(moved), *moved[0].shape), BF),
                pltpu.SemaphoreType.DMA((4 + 2 * len(moved) + len(shifts),)),
            ],
            compiler_params=params(56),
            cost_estimate=cost(2),
            name="dispatch",
        )(routes_t, gates_t, tokens, cotangent, *moved)

    def passed(value, estimate, *after):
        return pl.pallas_call(
            pass_kernel,
            out_shape=array(*value.shape),
            in_specs=[hbm()] * (1 + len(after)),
            out_specs=hbm(),
            input_output_aliases={0: 0},
            compiler_params=params(1),
            cost_estimate=cost(estimate),
            name="after",
        )(value, *after)

    shifts = list(range(experts))
    groups = [shifts[:-1], shifts[-1:]]
    own, sib = {}, {}
    relayed = experts == 4
    order = [1, 0] if relayed else shifts[1:] + [0]
    up_own, down_own, *sends = dispatch(order, up_weight[0], down_weight[0])
    for shift, send in zip(order, sends):
        own[shift] = shifted(send, shift) if shift else send
    if relayed:
        plan = shifted(jnp.concatenate([routes_t.astype(F32), gates_t]), 2)
        landed = shifted(tokens, 2)
        kept, on_x, cot = pl.pallas_call(
            functools.partial(relay_x_kernel, cap),
            out_shape=[array(cap, width)] * 2 + [array(rows, width)],
            in_specs=[vmem()] * 3,
            out_specs=[vmem()] * 3,
            compiler_params=params(12),
            cost_estimate=cost(1),
            name="relay_x",
        )(plan, landed, cotangent)
        far_x = shifted(on_x, 1)
        landed = shifted(cot, 2)
        own[2], on_s = pl.pallas_call(
            functools.partial(relay_s_kernel, cap),
            out_shape=[array(2 * cap, width), array(cap, width)],
            in_specs=[vmem()] * 4,
            out_specs=[vmem()] * 2,
            compiler_params=params(12),
            cost_estimate=cost(1),
            name="relay_s",
        )(plan, landed, kept, far_x)
        far_s = shifted(on_s, 1)
    else:
        far_x, far_s = own[experts - 1][:cap], own[experts - 1][cap:]
    for shift in groups[0]:
        sib[shift] = swapped(own[shift])

    def gathered(weight, order):
        blocks, layout, held = [weight], [[0]], [0]
        for bit in order:
            blocks.append(
                across(jnp.concatenate(blocks) if len(blocks) > 1 else weight, bit)
            )
            layout.append([peer ^ (1 << bit) for peer in held])
            held = held + layout[-1]
        return blocks, layout

    ups, up_layout = gathered(up_own, orders[0])
    downs, down_layout = gathered(down_own, orders[1])

    def chunk_call(kernel, group, chunks, operands, outs, name, estimate):
        count = len(group)
        parts = [array(count * cap, width)] * 2
        return pl.pallas_call(
            functools.partial(kernel[0], cap, count, *kernel[1:]),
            out_shape=parts + outs,
            in_specs=[vmem()] * (len(chunks) + len(operands)),
            out_specs=[vmem()] * (2 + len(outs)),
            scratch_shapes=[pltpu.VMEM((2 * count * cap, width), BF)] * 2,
            compiler_params=params(20),
            cost_estimate=cost(estimate),
            name=name,
        )(*chunks, *operands)

    total = jax.ShapeDtypeStruct((half, width), F32)
    part_own, part_sib, *held = chunk_call(
        (first_kernel, (up_layout, down_layout)),
        groups[0],
        [side[shift] for side in (own, sib) for shift in groups[0]],
        [*ups, *downs],
        [total, total, array(width, half), array(half, width), array(width, half)],
        "first",
        0.1,
    )
    halves = [(part_own, swapped(part_sib))]
    sums, weights = held[:2], held[2:]

    pairs, ready = {}, {}

    def paired(groups, halves, *after):
        counts = [len(group) for group in groups]
        results = pl.pallas_call(
            functools.partial(pair_kernel, cap, counts),
            out_shape=[array(cap, width)] * sum(counts),
            in_specs=[vmem()] * (2 * len(counts)) + [hbm()] * len(after),
            out_specs=[vmem()] * sum(counts),
            compiler_params=params(16),
            cost_estimate=cost(1),
            name="pair",
        )(*[value for both in halves for value in both], *after)
        for shift, result in zip([shift for group in groups for shift in group], results):
            ready[shift] = result
            pairs[shift] = shifted(result, shift) if shift else result

    paired(groups[:1], halves)

    far_s = passed(passed(far_s, 8), 0.1, part_own)
    last_chunk = [far_x, far_s, swapped(far_x), swapped(far_s)]

    def halving(order):
        kept = [0]
        for bit in order[::-1]:
            kept = [peer ^ (1 << bit) for peer in kept] + kept
        return kept

    cut = n_dp // 2
    grads = [array(cut * half, step)] + [array(half, step)] * cut
    part_own, part_sib, *results = chunk_call(
        (tail_kernel, halving(orders[0]), halving(orders[1])),
        groups[1],
        last_chunk,
        [*weights, *sums, ready[groups[0][-1]]],
        grads * 2,
        "tail",
        7,
    )
    up_grads, down_grads = results[: 1 + cut], results[1 + cut :]

    paired(groups[1:], [(part_own, swapped(part_sib))])

    grad_tokens, mark = pl.pallas_call(
        functools.partial(combine_kernel, experts, cap),
        out_shape=[array(rows, width), jax.ShapeDtypeStruct((8, 128), F32)],
        in_specs=[vmem()] * (1 + experts),
        out_specs=[vmem()] * 2,
        compiler_params=params(16),
        cost_estimate=cost(3),
        name="combine",
    )(routes_t, *[pairs[shift] for shift in range(experts)])

    def reduced(send, keeps, order, name):
        terms = [[(keep, 0)] for keep in keeps]
        for bit in order:
            landed = across(send, bit)
            for place in range(len(terms)):
                terms[place].append((landed, place))
            cut = len(terms) // 2
            if cut:
                sums = [
                    sum(
                        value[place * half : (place + 1) * half].astype(F32)
                        for value, place in block
                    ).astype(BF)
                    for block in terms[:cut]
                ]
                send = jnp.concatenate(sums) if cut > 1 else sums[0]
                terms = terms[cut:]
        (block,) = terms
        specs = [
            pl.BlockSpec((half, step), functools.partial(lambda place, i: (place, 0), place))
            for _, place in block
        ]
        return pl.pallas_call(
            functools.partial(last_kernel, len(block)),
            grid=(1,),
            out_shape=array(1, step, half),
            in_specs=specs + [pl.BlockSpec((8, 128), lambda i: (0, 0))],
            out_specs=pl.BlockSpec((1, step, half), lambda i: (0, 0, 0)),
            compiler_params=params(16),
            cost_estimate=cost(2),
            name=name,
        )(*[value for value, _ in block], mark)

    grad_up = reduced(up_grads[0], up_grads[1:], orders[0], "grad_up")
    grad_down = reduced(down_grads[0], down_grads[1:], orders[1], "grad_down")
    return (grad_tokens, grad_up, grad_down)


def solution(mesh):
    in_specs = (
        P(("dp", "expert"), None),
        P(("dp", "expert"), None),
        P(("dp", "expert"), None),
        P(("dp", "expert"), None),
        P("expert", "dp", None),
        P("expert", "dp", None),
    )
    out_specs = (P(("dp", "expert"), None), P("expert", "dp", None), P("expert", "dp", None))
    return jax.shard_map(
        functools.partial(on_device, mesh.shape["dp"], mesh.shape["expert"]),
        mesh=mesh,
        in_specs=in_specs,
        out_specs=out_specs,
        check_vma=False,
    )
```

```python
import functools

import jax
import jax.numpy as jnp
from jax import lax
from jax.experimental import pallas as pl
from jax.experimental.pallas import tpu as pltpu
from jax.sharding import PartitionSpec as P

BF = jnp.bfloat16
F32 = jnp.float32
MIB = 1024 * 1024


def vmem():
    return pl.BlockSpec(memory_space=pltpu.VMEM)


def hbm():
    return pl.BlockSpec(memory_space=pl.ANY)


def params(mebibytes):
    return pltpu.CompilerParams(vmem_limit_bytes=mebibytes * MIB)


def cost(microseconds):
    return pl.CostEstimate(
        flops=int(microseconds * 1.0e9), bytes_accessed=2**20, transcendentals=0
    )


def array(*shape):
    return jax.ShapeDtypeStruct(shape, BF)


def contract(a, b, da, db):
    return lax.dot_general(a, b, (((da,), (db,)), ((), ())), preferred_element_type=F32)


def slot_plan(routes):
    tokens = routes.shape[1]
    first, second = routes[0:1, :], routes[1:2, :]
    expert = lax.broadcasted_iota(jnp.int32, (128, tokens), 0)
    named = jnp.where((expert == first) | (expert == second), 1.0, 0.0).astype(BF)
    earlier = lax.broadcasted_iota(jnp.int32, (tokens, tokens), 0)
    later = lax.broadcasted_iota(jnp.int32, (tokens, tokens), 1)
    place = contract(named, jnp.where(earlier < later, 1.0, 0.0).astype(BF), 1, 0)
    return first, second, expert, place


def slot_masks(plan, chosen, cap):
    first, second, expert, place = plan
    own = jnp.sum(jnp.where(expert == chosen, place, 0.0), axis=0, keepdims=True)
    slot = lax.broadcasted_iota(jnp.int32, (cap, first.shape[1]), 0)
    here = slot == own.astype(jnp.int32)
    return here & (first == chosen), here & (second == chosen)


def slot_pick(plan, gates, chosen, cap):
    mask0, mask1 = slot_masks(plan, chosen, cap)
    gate = jnp.sum(
        jnp.where(mask0, gates[0:1, :], 0.0) + jnp.where(mask1, gates[1:2, :], 0.0),
        axis=1,
        keepdims=True,
    )
    return jnp.where(mask0 | mask1, 1.0, 0.0).astype(BF), gate


def relay_x_kernel(cap, plan_ref, tok_ref, cot_ref, keep_ref, on_ref, cot_out):
    chip = lax.axis_index("expert") // 2
    values = plan_ref[...]
    plan = slot_plan(values[0:2, :].astype(jnp.int32))
    for chosen, out in ((chip, keep_ref), (chip ^ 1, on_ref)):
        pick, _ = slot_pick(plan, values[2:4, :], chosen, cap)
        out[...] = contract(pick, tok_ref[...], 1, 0).astype(BF)
    cot_out[...] = cot_ref[...]


def relay_s_kernel(cap, plan_ref, cot_ref, kept_ref, named_ref, keep_ref, on_ref):
    chip = lax.axis_index("expert") // 2
    values = plan_ref[...]
    plan = slot_plan(values[0:2, :].astype(jnp.int32))
    keep_ref[:cap, :] = kept_ref[...]
    for chosen, out, start in ((chip, keep_ref, cap), (chip ^ 1, on_ref, 0)):
        pick, gate = slot_pick(plan, values[2:4, :], chosen, cap)
        out[start : start + cap, :] = (gate * contract(pick, cot_ref[...], 1, 0)).astype(BF)


def dispatch_kernel(experts, cap, shifts, moved, *refs):
    refs = list(refs)
    sources, refs = refs[: 4 + moved], refs[4 + moved :]
    moved_outs, outs, refs = refs[:moved], refs[moved : moved + len(shifts)], refs[moved + len(shifts) :]
    routes_ref, gates_ref, tok_ref, cot_ref, made, held, sems = refs
    landings = [routes_ref, gates_ref, tok_ref, cot_ref] + [held.at[i] for i in range(moved)]
    copies = []

    def copy(source, landing):
        copies.append(pltpu.make_async_copy(source, landing, sems.at[len(copies)]))
        copies[-1].start()

    for source, landing in zip(sources, landings):
        copy(source, landing)
    for one in copies[:2]:
        one.wait()
    chip = lax.axis_index("expert") // 2
    plan = slot_plan(routes_ref[...])
    gates = gates_ref[...]
    for one in copies[2:4]:
        one.wait()
    for index, shift in enumerate(shifts):
        pick, gate = slot_pick(plan, gates, chip ^ shift, cap)
        made[index, :cap, :] = contract(pick, tok_ref[...], 1, 0).astype(BF)
        made[index, cap:, :] = (gate * contract(pick, cot_ref[...], 1, 0)).astype(BF)
        copy(made.at[index], outs[index])
    for index in range(moved):
        copies[4 + index].wait()
        copy(held.at[index], moved_outs[index])
    for one in copies[4 + moved :]:
        one.wait()


def combine_kernel(experts, cap, routes_ref, *rest):
    backs, out_ref, mark_ref = rest[:-2], rest[-2], rest[-1]
    mark_ref[...] = jnp.zeros_like(mark_ref)
    chip = lax.axis_index("expert") // 2
    plan = slot_plan(routes_ref[...])
    picks = []
    for shift in range(experts):
        mask0, mask1 = slot_masks(plan, chip ^ shift, cap)
        picks.append(jnp.where(mask0 | mask1, 1.0, 0.0).astype(BF).T)
    width = out_ref.shape[1]
    tile = 640
    for start in range(0, width, tile):
        cols = slice(start, start + tile)
        total = None
        for shift in range(experts):
            term = contract(picks[shift], backs[shift][:, cols], 1, 0)
            total = term if total is None else total + term
        out_ref[:, cols] = total.astype(BF)


def chunk_rows(cap, owns, sibs, rows_x, rows_s):
    for index, block in enumerate(list(owns) + list(sibs)):
        place = slice(index * cap, (index + 1) * cap)
        rows_x[place, :] = block[:cap, :]
        rows_s[place, :] = block[cap:, :]


def expert_work(rows_x, rows_s, up, down):
    hidden = contract(rows_x[...], up[...], 1, 0)
    sig = jax.nn.sigmoid(hidden)
    active = (hidden * sig).astype(BF)
    slope = sig * (1.0 + hidden * (1.0 - sig))
    back_hidden = (contract(rows_s[...], down[...], 1, 0) * slope).astype(BF)
    return active, back_hidden


def tiles(width):
    tile = 512 if width % 512 == 0 else 128
    return [slice(start, start + tile) for start in range(0, width, tile)]


def partial_rows(back_hidden, up_turned, part_own, part_sib):
    half_rows = part_own.shape[0]
    for cols in tiles(part_own.shape[1]):
        part = contract(back_hidden, up_turned[:, cols], 1, 0).astype(BF)
        part_own[:, cols] = part[:half_rows]
        part_sib[:, cols] = part[half_rows:]


def first_kernel(cap, count, layout, *refs):
    owns, sibs, refs = refs[:count], refs[count : 2 * count], refs[2 * count :]
    n_up, n_down = len(layout[0]), len(layout[1])
    ups, downs = refs[:n_up], refs[n_up : n_up + n_down]
    refs = refs[n_up + n_down :]
    part_own, part_sib, sum_up, sum_down, up, up_turned, down, rows_x, rows_s = refs
    step = ups[0].shape[0]
    me = lax.axis_index("dp")
    for full, lay, blocks in ((up, layout[0], ups), (down, layout[1], downs)):
        for peers, block in zip(lay, blocks):
            for place, peer in enumerate(peers):
                home = pl.ds(pl.multiple_of((me ^ peer) * step, 16), step)
                full[home, :] = block[place * step : (place + 1) * step, :]
    up_turned[...] = up[...].T
    chunk_rows(cap, owns, sibs, rows_x, rows_s)
    active, back_hidden = expert_work(rows_x, rows_s, up, down)
    partial_rows(back_hidden, up_turned, part_own, part_sib)
    for units, rows, total in ((active, rows_s, sum_down), (back_hidden, rows_x, sum_up)):
        turned = units.T
        for cols in tiles(total.shape[1]):
            total[:, cols] = contract(turned, rows[:, cols], 1, 0)


def tail_kernel(cap, count, order_up, order_down, *refs):
    x_own, s_own, x_sib, s_sib = refs[:4]
    refs = refs[4:]
    up, up_turned, down, up_in, down_in = refs[:5]
    refs = refs[6:]
    part_own, part_sib = refs[:2]
    cut = len(order_up) // 2
    up_outs, down_outs = refs[2 : 3 + cut], refs[3 + cut : 4 + 2 * cut]
    rows_x, rows_s = refs[4 + 2 * cut :]
    half, step = up_outs[1].shape
    me = lax.axis_index("dp")
    for rows, own, sib in ((rows_x, x_own, x_sib), (rows_s, s_own, s_sib)):
        rows[:cap, :] = own[...]
        rows[cap:, :] = sib[...]
    active, back_hidden = expert_work(rows_x, rows_s, up, down)
    for units, rows, before, order, outs in (
        (active, rows_s, down_in, order_down, down_outs),
        (back_hidden, rows_x, up_in, order_up, up_outs),
    ):
        turned = units.T
        for place, peer in enumerate(order):
            cols = pl.ds(pl.multiple_of((me ^ peer) * step, 128), step)
            block = (before[:, cols] + contract(turned, rows[:, cols], 1, 0)).astype(BF)
            if place < cut:
                outs[0][place * half : (place + 1) * half, :] = block
            else:
                outs[1 + place - cut][...] = block
    partial_rows(back_hidden, up_turned, part_own, part_sib)


def pair_kernel(cap, counts, *refs):
    outs = refs[len(refs) - sum(counts) :]
    place = 0
    for group, count in enumerate(counts):
        own_ref, other_ref = refs[2 * group : 2 * group + 2]
        for index in range(count):
            rows = slice(index * cap, (index + 1) * cap)
            outs[place][...] = (
                own_ref[rows, :].astype(F32) + other_ref[rows, :].astype(F32)
            ).astype(BF)
            place += 1


def pass_kernel(*refs):
    pass


def last_kernel(count, *refs):
    total = refs[0][...].astype(F32)
    for term in refs[1:count]:
        total = total + term[...].astype(F32)
    refs[-1][0] = total.T.astype(BF)


def on_device(n_dp, n_expert, tokens, cotangent, routes, gate_values, up_weight, down_weight):
    rows, width = tokens.shape
    top = routes.shape[1]
    experts = n_expert // 2
    cap = -(-(5 * rows * top // (4 * experts)) // 16) * 16
    step, half = up_weight.shape[1:]
    bits = n_dp.bit_length() - 1
    orders = (list(range(bits)), list(range(bits))[::-1])

    def shifted(value, shift):
        pairs = [(2 * z + c, 2 * (z ^ shift) + c) for z in range(experts) for c in range(2)]
        return lax.ppermute(value, "expert", pairs)

    def swapped(value):
        return lax.ppermute(value, "expert", [(i, i ^ 1) for i in range(n_expert)])

    def across(value, bit):
        return lax.ppermute(value, "dp", [(d, d ^ (1 << bit)) for d in range(n_dp)])

    routes_t, gates_t = routes.T, gate_values.T

    def dispatch(shifts, *moved):
        return pl.pallas_call(
            functools.partial(dispatch_kernel, experts, cap, shifts, len(moved)),
            out_shape=[array(*value.shape) for value in moved]
            + [array(2 * cap, width)] * len(shifts),
            in_specs=[hbm()] * (4 + len(moved)),
            out_specs=[hbm()] * (len(moved) + len(shifts)),
            scratch_shapes=[
                pltpu.VMEM(routes_t.shape, routes_t.dtype),
                pltpu.VMEM(gates_t.shape, gates_t.dtype),
                pltpu.VMEM(tokens.shape, BF),
                pltpu.VMEM(cotangent.shape, BF),
                pltpu.VMEM((len(shifts), 2 * cap, width), BF),
                pltpu.VMEM((len(moved), *moved[0].shape), BF),
                pltpu.SemaphoreType.DMA((4 + 2 * len(moved) + len(shifts),)),
            ],
            compiler_params=params(56),
            cost_estimate=cost(2),
            name="dispatch",
        )(routes_t, gates_t, tokens, cotangent, *moved)

    def passed(value, estimate, *after):
        return pl.pallas_call(
            pass_kernel,
            out_shape=array(*value.shape),
            in_specs=[hbm()] * (1 + len(after)),
            out_specs=hbm(),
            input_output_aliases={0: 0},
            compiler_params=params(1),
            cost_estimate=cost(estimate),
            name="after",
        )(value, *after)

    shifts = list(range(experts))
    groups = [shifts[:-1], shifts[-1:]]
    own, sib = {}, {}
    relayed = experts == 4
    order = [1, 0] if relayed else shifts[1:] + [0]
    up_own, down_own, *sends = dispatch(order, up_weight[0], down_weight[0])
    sends = dict(zip(order, sends))
    for shift in order:
        if shift != 1:
            own[shift] = shifted(sends[shift], shift) if shift else sends[shift]
    if relayed:
        plan = shifted(jnp.concatenate([routes_t.astype(F32), gates_t]), 2)
        landed = shifted(tokens, 2)
        kept, on_x, cot = pl.pallas_call(
            functools.partial(relay_x_kernel, cap),
            out_shape=[array(cap, width)] * 2 + [array(rows, width)],
            in_specs=[vmem()] * 3,
            out_specs=[vmem()] * 3,
            compiler_params=params(12),
            cost_estimate=cost(1),
            name="relay_x",
        )(plan, landed, cotangent)
        far_x = shifted(on_x, 1)
        landed = shifted(cot, 2)
        own[2], on_s = pl.pallas_call(
            functools.partial(relay_s_kernel, cap),
            out_shape=[array(2 * cap, width), array(cap, width)],
            in_specs=[vmem()] * 4,
            out_specs=[vmem()] * 2,
            compiler_params=params(12),
            cost_estimate=cost(1),
            name="relay_s",
        )(plan, landed, kept, far_x)
        far_s = shifted(on_s, 1)
    else:
        far_x, far_s = own[experts - 1][:cap], own[experts - 1][cap:]
    def gathered(weight, order):
        blocks, layout, held = [weight], [[0]], [0]
        for bit in order:
            blocks.append(
                across(jnp.concatenate(blocks) if len(blocks) > 1 else weight, bit)
            )
            layout.append([peer ^ (1 << bit) for peer in held])
            held = held + layout[-1]
        return blocks, layout

    ups, up_layout = gathered(up_own, orders[0])
    downs, down_layout = gathered(down_own, orders[1])
    own[1] = shifted(passed(sends[1], 0.1, ups[1]), 1)
    for shift in groups[0]:
        sib[shift] = swapped(own[shift])
    ups[-1], downs[-1] = passed(ups[-1], 3), passed(downs[-1], 3)

    def chunk_call(kernel, group, chunks, operands, outs, name, estimate):
        count = len(group)
        parts = [array(count * cap, width)] * 2
        return pl.pallas_call(
            functools.partial(kernel[0], cap, count, *kernel[1:]),
            out_shape=parts + outs,
            in_specs=[vmem()] * (len(chunks) + len(operands)),
            out_specs=[vmem()] * (2 + len(outs)),
            scratch_shapes=[pltpu.VMEM((2 * count * cap, width), BF)] * 2,
            compiler_params=params(20),
            cost_estimate=cost(estimate),
            name=name,
        )(*chunks, *operands)

    total = jax.ShapeDtypeStruct((half, width), F32)
    part_own, part_sib, *held = chunk_call(
        (first_kernel, (up_layout, down_layout)),
        groups[0],
        [side[shift] for side in (own, sib) for shift in groups[0]],
        [*ups, *downs],
        [total, total, array(width, half), array(half, width), array(width, half)],
        "first",
        0.1,
    )
    halves = [(part_own, swapped(part_sib))]
    sums, weights = held[:2], held[2:]

    pairs, ready = {}, {}

    def paired(groups, halves, *after):
        counts = [len(group) for group in groups]
        results = pl.pallas_call(
            functools.partial(pair_kernel, cap, counts),
            out_shape=[array(cap, width)] * sum(counts),
            in_specs=[vmem()] * (2 * len(counts)) + [hbm()] * len(after),
            out_specs=[vmem()] * sum(counts),
            compiler_params=params(16),
            cost_estimate=cost(1),
            name="pair",
        )(*[value for both in halves for value in both], *after)
        for shift, result in zip([shift for group in groups for shift in group], results):
            ready[shift] = result
            pairs[shift] = shifted(result, shift) if shift else result

    paired(groups[:1], halves)

    far_s = passed(passed(far_s, 8), 0.1, part_own)
    last_chunk = [far_x, far_s, swapped(far_x), swapped(far_s)]

    def halving(order):
        kept = [0]
        for bit in order[::-1]:
            kept = [peer ^ (1 << bit) for peer in kept] + kept
        return kept

    cut = n_dp // 2
    grads = [array(cut * half, step)] + [array(half, step)] * cut
    part_own, part_sib, *results = chunk_call(
        (tail_kernel, halving(orders[0]), halving(orders[1])),
        groups[1],
        last_chunk,
        [*weights, *sums, ready[groups[0][-1]]],
        grads * 2,
        "tail",
        7,
    )
    up_grads, down_grads = results[: 1 + cut], results[1 + cut :]

    paired(groups[1:], [(part_own, swapped(part_sib))])

    grad_tokens, mark = pl.pallas_call(
        functools.partial(combine_kernel, experts, cap),
        out_shape=[array(rows, width), jax.ShapeDtypeStruct((8, 128), F32)],
        in_specs=[vmem()] * (1 + experts),
        out_specs=[vmem()] * 2,
        compiler_params=params(16),
        cost_estimate=cost(3),
        name="combine",
    )(routes_t, *[pairs[shift] for shift in range(experts)])

    def reduced(send, keeps, order, name):
        terms = [[(keep, 0)] for keep in keeps]
        for bit in order:
            landed = across(send, bit)
            for place in range(len(terms)):
                terms[place].append((landed, place))
            cut = len(terms) // 2
            if cut:
                sums = [
                    sum(
                        value[place * half : (place + 1) * half].astype(F32)
                        for value, place in block
                    ).astype(BF)
                    for block in terms[:cut]
                ]
                send = jnp.concatenate(sums) if cut > 1 else sums[0]
                terms = terms[cut:]
        (block,) = terms
        specs = [
            pl.BlockSpec((half, step), functools.partial(lambda place, i: (place, 0), place))
            for _, place in block
        ]
        return pl.pallas_call(
            functools.partial(last_kernel, len(block)),
            grid=(1,),
            out_shape=array(1, step, half),
            in_specs=specs + [pl.BlockSpec((8, 128), lambda i: (0, 0))],
            out_specs=pl.BlockSpec((1, step, half), lambda i: (0, 0, 0)),
            compiler_params=params(16),
            cost_estimate=cost(2),
            name=name,
        )(*[value for value, _ in block], mark)

    grad_up = reduced(up_grads[0], up_grads[1:], orders[0], "grad_up")
    grad_down = reduced(down_grads[0], down_grads[1:], orders[1], "grad_down")
    return (grad_tokens, grad_up, grad_down)


def solution(mesh):
    in_specs = (
        P(("dp", "expert"), None),
        P(("dp", "expert"), None),
        P(("dp", "expert"), None),
        P(("dp", "expert"), None),
        P("expert", "dp", None),
        P("expert", "dp", None),
    )
    out_specs = (P(("dp", "expert"), None), P("expert", "dp", None), P("expert", "dp", None))
    return jax.shard_map(
        functools.partial(on_device, mesh.shape["dp"], mesh.shape["expert"]),
        mesh=mesh,
        in_specs=in_specs,
        out_specs=out_specs,
        check_vma=False,
    )
```
